32 devices in a mesh: dp: 4 (over y, x), expert: 8 (over z, core).
Axes of the slice: x: 2, y: 2, z: 4, core: 2. Of those that a mesh axis runs over, the one named last changes fastest.
Arguments:
- tokens: bfloat16 [1024, 4096], P('expert', 'dp'), may hold values from -6 to 6
- routes: int32 [1024, 4], P('expert'), may hold values from 0 to 7, all different within a row; in each aligned block of 128 rows (0 to 127, 128 to 255, ...) at most 128 rows name the same one
- route_weights: float32 [1024, 4], P('expert'), may hold values from 0.1 to 1
- gate_weight: bfloat16 [8, 4096, 1536], P('expert', None, 'dp'), may hold values from -0.09375 to 0.09375
- up_weight: bfloat16 [8, 4096, 1536], P('expert', None, 'dp'), may hold values from -0.09375 to 0.09375
- down_weight: bfloat16 [8, 1536, 4096], P('expert', 'dp'), may hold values from -0.15625 to 0.15625
- sketch_basis: bfloat16 [1536, 128], P('dp'), may hold values from -0.15625 to 0.15625
Outputs:
- mixed: bfloat16 [1024, 4096], P('expert', 'dp')
- sketch: float32 [8, 128, 1536], P('expert', None, 'dp')
The draws below stay inside these ranges and needn't reach their ends.
Inputs may be any that keep to these rules, and one draw needn't show every extreme that they name: `routes`: each row names 4 different experts; within the rows of one device no expert is named more than 128 times, a bound that some block reaches.
All inputs are finite; a program needn't handle non-finite values.
Results may differ from the reference program's by a relative error of at most 0.017.
Values may be sent and summed in bfloat16 or wider, within the bound.
A program may use at most 128 MiB of HBM per device.

```python
import math
import jax
import jax.numpy as jnp
import numpy as np
from jax import lax

D = 4096
FF = 1536
TOP = 4
SK = 128
TOK_DEV = 128
EXPERTS = 8
FF_DEV = 384
CAP = 128
TOKENS = 1024
N_DP = 4
N_EXPERT = 8


def level_of(rng, shape, shards, low, high):
    factor_of = 1.0
    for axis_at, blocks in shards:
        steps = jax.random.uniform(jax.random.fold_in(jax.random.fold_in(rng, 6), axis_at), (blocks,), jnp.float32, low / len(shards), high / len(shards))
        factor_of = factor_of * jnp.repeat(jnp.exp(steps), shape[axis_at] // blocks).reshape((-1,) + (1,) * (len(shape) - 1 - axis_at))
    return factor_of


def routed_block(rng, own, number, rows, number_of, top, bound, skew):
    ranking = jax.random.permutation(rng, number_of)
    heavy_load, common = load_shares(number_of, rows * top, bound, skew, True), load_shares(number_of, rows * top, bound, skew, False)
    places = jnp.arange(number_of)

    def named(sizes, turn):
        used = int((sizes > 0).sum())
        fixed = max(1, used // 4)
        passed = fixed + (places - fixed + turn * (used - fixed)) % max(1, number_of - fixed)
        return jnp.zeros((number_of,), jnp.int32).at[ranking[jnp.where(places < fixed, places, passed)]].set(jnp.asarray(sizes, jnp.int32))

    sizes = jnp.where(number % 4 == 0, named(heavy_load, number // 4), named(common, number - number // 4 - 1))
    mixed = jax.random.permutation(jax.random.fold_in(own, 3), number_of)
    source_of, taker = mixed[0:number_of // 2 * 2:2], mixed[1:number_of // 2 * 2:2]
    slack = jnp.minimum(sizes[source_of] - 1, bound - sizes[taker]) // 2
    slack = jnp.where((source_of == ranking[0]) | (taker == ranking[0]) | (sizes[taker] == 0), 0, jnp.maximum(slack, 0))
    passed = jax.random.randint(jax.random.fold_in(own, 4), (number_of // 2,), 0, 1 << 20) % (slack + 1)
    sizes = sizes.at[source_of].add(-passed).at[taker].add(passed)
    members = jnp.searchsorted(jnp.cumsum(sizes), jnp.arange(rows * top), side="right").astype(jnp.int32)
    table = members.reshape(top, rows).T
    table = table[jax.random.permutation(jax.random.fold_in(own, 1), rows)]
    turn = jax.random.randint(jax.random.fold_in(own, 2), (rows, 1), 0, top)
    return jnp.take_along_axis(table, (jnp.arange(top)[None, :] + turn) % top, axis=1)


def load_shares(number_of, total, limit, slope, full):
    portions = [(1 << 20) // math.isqrt(standing ** slope) + 1 for standing in range(1, number_of + 1)]
    largest = limit if full else min(limit, max(-(-total // number_of), total * portions[0] // sum(portions)))
    least = 1 if total - largest >= number_of - 1 else 0
    holding, spare = [largest] + [least] * (number_of - 1), total - largest - least * (number_of - 1)
    while spare > 0:
        candidates = [i for i in range(1, number_of) if holding[i] < largest] or [i for i in range(1, number_of) if holding[i] < limit]
        mass, remaining = sum([portions[i] for i in candidates]), spare
        for i in candidates:
            extra = min(limit - holding[i], max(1, remaining * portions[i] // mass), spare)
            holding[i] = holding[i] + extra
            spare = spare - extra
    return np.array(holding)


def normal_values(rng, shape, deviation, bound, split=(), kind=jnp.bfloat16):
    level = level_of(rng, shape, split, -0.22, 0.18) if split else 1.0
    entries = jax.random.normal(rng, shape, jnp.float32) * deviation * level
    return jnp.minimum(jnp.maximum(entries, -bound), bound).astype(kind)


def setup_inputs(seed: int = 0) -> dict:
    key_of = jax.random.split(jax.random.key(seed), 8)
    tokens = normal_values(key_of[0], (TOKENS, D), 1.0, 6.0, ((0, 8), (1, 4)))
    routes_keys = jax.random.split(jax.random.fold_in(key_of[1], 1), TOKENS // TOK_DEV)
    routes_turns = jax.random.permutation(jax.random.fold_in(key_of[1], 3), TOKENS // TOK_DEV)
    routes = jax.vmap(lambda own, number: routed_block(jax.random.fold_in(key_of[1], 2), own, number, TOK_DEV, EXPERTS, TOP, CAP, 2))(routes_keys, routes_turns).reshape((TOKENS, TOP))
    route_weights = jnp.clip(0.1 + 0.9 * jax.random.uniform(key_of[2], (TOKENS, TOP), jnp.float32) ** level_of(key_of[2], (TOKENS, TOP), ((0, 8),), -0.2, 0.2), 0.1, 1.0)
    gate_weight = normal_values(key_of[3], (EXPERTS, D, FF), D ** -0.5, 0.09375, ((0, 8), (2, 4)))
    up_weight = normal_values(key_of[4], (EXPERTS, D, FF), D ** -0.5, 0.09375, ((0, 8), (2, 4)))
    down_weight = normal_values(key_of[5], (EXPERTS, FF, D), FF ** -0.5, 0.15625, ((0, 8), (1, 4)))
    sketch_basis = normal_values(key_of[6], (FF, SK), FF ** -0.5, 0.15625, ((0, 4),))
    return {"tokens": tokens, "routes": routes, "route_weights": route_weights, "gate_weight": gate_weight, "up_weight": up_weight, "down_weight": down_weight, "sketch_basis": sketch_basis}


ridge_term = 1.0

def reference(tokens, routes, route_weights, gate_weight, up_weight, down_weight, sketch_basis):
    route_list = routes.reshape(-1)
    order_list = jnp.argsort(route_list, stable=True).astype(jnp.int32)
    row_limit = N_EXPERT * CAP
    padded_order = jnp.concatenate([order_list, jnp.zeros((row_limit,), jnp.int32)])
    onehot = (route_list[:, None] == jnp.arange(EXPERTS, dtype=jnp.int32)[None, :]).astype(jnp.int32)
    expert_counts = jnp.sum(onehot, axis=0).astype(jnp.int32)
    expert_starts = (jnp.cumsum(expert_counts) - expert_counts).astype(jnp.int32)
    weight_list = route_weights.reshape(-1)
    block_rows = min(256, row_limit)
    eye_matrix = jnp.eye(SK, dtype=jnp.float32)

    def per_expert(accum, inputs):
        begin_at, live_total, gate_expert, up_expert, down_expert = inputs
        pair_rows = lax.dynamic_slice_in_dim(padded_order, begin_at, row_limit, 0)

        def one_block(block_index, state):
            mixed_acc, gram_acc, proj_acc = state
            offset = block_index * block_rows
            pair_block = lax.dynamic_slice_in_dim(pair_rows, offset, block_rows, 0)
            alive = offset + jnp.arange(block_rows, dtype=jnp.int32) < live_total
            token_ids = pair_block // TOP
            chosen = jnp.where(alive[:, None], tokens[token_ids], jnp.zeros((), tokens.dtype))
            gate_val = jnp.dot(chosen.astype(jnp.float32), gate_expert.astype(jnp.float32), preferred_element_type=jnp.float32)
            up_val = jnp.dot(chosen.astype(jnp.float32), up_expert.astype(jnp.float32), preferred_element_type=jnp.float32)
            hidden = (jax.nn.silu(gate_val) * up_val).astype(jnp.bfloat16)
            summed = jnp.zeros((block_rows, D), jnp.float32)
            for quarter in range(N_DP):
                lower_unit = quarter * FF_DEV
                part = jnp.dot(hidden[:, lower_unit:lower_unit + FF_DEV].astype(jnp.float32), down_expert[lower_unit:lower_unit + FF_DEV, :].astype(jnp.float32), preferred_element_type=jnp.float32).astype(jnp.bfloat16)
                summed = summed + part.astype(jnp.float32)
            expert_out = summed.astype(jnp.bfloat16)
            pair_weight = jnp.where(alive, weight_list[pair_block], 0.0)
            mixed_acc = mixed_acc.at[token_ids].add(pair_weight[:, None] * expert_out.astype(jnp.float32))
            sketch_rows = jnp.dot(hidden.astype(jnp.float32), sketch_basis.astype(jnp.float32), preferred_element_type=jnp.float32)
            gram_acc = gram_acc + jnp.dot(sketch_rows.T, sketch_rows, precision=lax.Precision.HIGHEST)
            proj_acc = proj_acc + jnp.dot(sketch_rows.T, hidden.astype(jnp.float32), precision=lax.Precision.HIGHEST)
            return (mixed_acc, gram_acc, proj_acc)
        block_count = (live_total + block_rows - 1) // block_rows
        start_state = (accum, jnp.zeros((SK, SK), jnp.float32), jnp.zeros((SK, FF), jnp.float32))
        accum, gram_total, proj_total = lax.fori_loop(0, block_count, one_block, start_state)
        lower_factor = jnp.linalg.cholesky(gram_total + ridge_term * eye_matrix)
        whitened = jax.scipy.linalg.solve_triangular(lower_factor, proj_total, lower=True)
        return (accum, whitened)
    start_accum = jnp.zeros((TOKENS, D), jnp.float32)
    mixed_total, sketches = lax.scan(per_expert, start_accum, (expert_starts, expert_counts, gate_weight, up_weight, down_weight))
    return (mixed_total.astype(jnp.bfloat16), sketches)
```

```python
import jax
import jax.numpy as jnp
from jax import lax
from jax.experimental import pallas as pl
from jax.experimental.pallas import tpu as pltpu
from jax.sharding import PartitionSpec as P

MESH = pl.DeviceIdType.MESH
VMEM_BYTES = 56 * 1024 * 1024

ridge_term = 1.0


def gram_matrix(factor_rows):
    return jnp.dot(factor_rows.T, factor_rows, precision=lax.Precision.HIGHEST)


def body(tokens, routes, route_weights, gate_weight, up_weight, down_weight, sketch_basis):
    owners = lax.axis_size("expert")
    token_count, route_count = routes.shape
    pair_count = token_count * route_count
    capacity = 2 * pair_count // owners
    slot_total = owners * capacity
    route_list = routes.reshape(-1)
    onehot = (route_list[:, None] == jnp.arange(owners, dtype=jnp.int32)[None, :]).astype(jnp.int32)
    before = jnp.cumsum(onehot, axis=0) - onehot
    slot_of = jnp.sum(before * onehot, axis=1)
    counts = jnp.sum(onehot, axis=0)
    target = route_list * capacity + slot_of
    source_pair = (
        jnp.zeros((slot_total,), jnp.int32).at[target].set(jnp.arange(pair_count, dtype=jnp.int32))
    )
    source_token = source_pair // route_count
    count_wire = counts.astype(jnp.bfloat16)
    features = lax.all_gather(tokens, "dp", axis=1, tiled=True)
    outgoing = features[source_token].reshape(owners, capacity, features.shape[1])
    arrived, arrived_counts = (
        lax.all_to_all(outgoing, "expert", split_axis=0, concat_axis=0, tiled=True),
        lax.all_to_all(count_wire, "expert", split_axis=0, concat_axis=0, tiled=True),
    )
    width = arrived.shape[2]
    live_count = arrived_counts.astype(jnp.int32)
    live_mask = (jnp.arange(capacity, dtype=jnp.int32)[None, :] < live_count[:, None]).reshape(-1)
    slot_rows = jnp.where(
        live_mask[:, None], arrived.reshape(slot_total, width), jnp.zeros((), jnp.bfloat16)
    )
    gate_local = gate_weight[0]
    up_local = up_weight[0]
    down_local = down_weight[0]
    gate_val = jnp.dot(slot_rows, gate_local, preferred_element_type=jnp.float32)
    up_val = jnp.dot(slot_rows, up_local, preferred_element_type=jnp.float32)
    hidden_block = (jax.nn.silu(gate_val) * up_val).astype(jnp.bfloat16)
    partial_value = jnp.dot(hidden_block, down_local, preferred_element_type=jnp.float32)
    sums = lax.psum_scatter(
        partial_value.reshape(owners, capacity, width).astype(jnp.bfloat16),
        "dp",
        scatter_dimension=2,
        tiled=True,
    )
    returned = lax.all_to_all(sums, "expert", split_axis=0, concat_axis=0, tiled=True)
    picked = returned.reshape(slot_total, returned.shape[2])[target]
    weighted = jnp.einsum(
        "tkd,tk->td",
        picked.reshape(token_count, route_count, returned.shape[2]).astype(jnp.float32),
        route_weights,
    )
    mixed = weighted.astype(jnp.bfloat16)
    sketch_part = jnp.dot(hidden_block, sketch_basis, preferred_element_type=jnp.float32)
    sketch_width = sketch_part.shape[1]
    eye_matrix = jnp.eye(sketch_width, dtype=jnp.float32)
    sketch_full = lax.psum(sketch_part.astype(jnp.bfloat16), "dp").astype(jnp.float32)
    lower_factor = jnp.linalg.cholesky(gram_matrix(sketch_full) + ridge_term * eye_matrix)
    projected = jnp.dot(
        sketch_full.T, hidden_block.astype(jnp.float32), precision=lax.Precision.HIGHEST
    )
    whitened = jax.scipy.linalg.solve_triangular(lower_factor, projected, lower=True)
    return (mixed, whitened[None])


def place():
    dp, expert = lax.axis_index("dp"), lax.axis_index("expert")
    y, x = dp // 2, dp % 2
    z, core = expert // 2, expert % 2
    return dp, expert, y, x, z, core


def enter(partners):
    barrier = pltpu.get_barrier_semaphore()
    for partner in partners:
        pl.semaphore_signal(barrier, inc=1, device_id=partner, device_id_type=MESH)
    pl.semaphore_wait(barrier, len(partners))


def gather_kernel(tok_ref, out_ref, own_sem, z_send, z_recv, x_send, x_recv, y_send, y_recv, dx_send, dx_recv, dy_send, dy_recv, s_send, s_recv):
    dp, expert, y, x, z, core = place()
    rows, cols = tok_ref.shape
    half = rows // 2
    x_dp, y_dp, d_dp = y * 2 + 1 - x, (1 - y) * 2 + x, (1 - y) * 2 + 1 - x
    other = (dp, z * 2 + 1 - core)
    x_dev, y_dev = (x_dp, expert), (y_dp, expert)
    z_devs = [(dp, (z + k) % 4 * 2 + core) for k in range(1, 4)]
    enter([other, x_dev, y_dev] + z_devs)

    def block(dp_at, k, low=0, count=rows):
        at = ((z + 4 - k) % 4 * 2 + core) * rows + low
        return out_ref.at[pl.ds(at, count), pl.ds(dp_at * cols, cols)]

    def copy(ref, dst, send, recv, device):
        return pltpu.make_async_remote_copy(
            src_ref=ref, dst_ref=dst, send_sem=send, recv_sem=recv, device_id=device, device_id_type=MESH
        )

    sent = []

    def go(*args):
        c = copy(*args)
        c.start()
        sent.append(c)

    def arrived(dst, send, recv):
        copy(dst, dst, send, recv, other).wait_recv()

    own = pltpu.make_async_copy(tok_ref, block(dp, 0), own_sem)
    own.start()
    go(tok_ref, block(dp, 0), x_send.at[0], x_recv.at[0], x_dev)
    go(tok_ref, block(dp, 0), y_send.at[0], y_recv.at[0], y_dev)
    for k in range(1, 4):
        go(tok_ref, block(dp, 0), z_send.at[k - 1], z_recv.at[k - 1], z_devs[k - 1])
    go(tok_ref, block(dp, 0), s_send.at[0], s_recv.at[0], other)

    def near(k):
        arrived(block(x_dp, k), x_send.at[k], x_recv.at[k])
        go(block(x_dp, k, 0, half), block(x_dp, k, 0, half), dy_send.at[k], dy_recv.at[k], y_dev)
        go(block(x_dp, k), block(x_dp, k), s_send.at[4 + k], s_recv.at[4 + k], other)
        arrived(block(y_dp, k), y_send.at[k], y_recv.at[k])
        go(block(y_dp, k, half, half), block(y_dp, k, half, half), dx_send.at[k], dx_recv.at[k], x_dev)
        go(block(y_dp, k), block(y_dp, k), s_send.at[8 + k], s_recv.at[8 + k], other)

    def far(k):
        arrived(block(d_dp, k, 0, half), dy_send.at[k], dy_recv.at[k])
        arrived(block(d_dp, k, half, half), dx_send.at[k], dx_recv.at[k])
        go(block(d_dp, k), block(d_dp, k), s_send.at[12 + k], s_recv.at[12 + k], other)

    def column(k):
        arrived(block(dp, k), z_send.at[k - 1], z_recv.at[k - 1])
        go(block(dp, k), block(dp, k), x_send.at[k], x_recv.at[k], x_dev)
        go(block(dp, k), block(dp, k), y_send.at[k], y_recv.at[k], y_dev)
        go(block(dp, k), block(dp, k), s_send.at[k], s_recv.at[k], other)

    column(1)
    near(0)
    column(3)
    column(2)
    near(1)
    far(0)
    near(3)
    far(1)
    near(2)
    far(3)
    far(2)
    for j, dp_at in enumerate((dp, x_dp, y_dp, d_dp)):
        for k in range(4):
            at = ((z + 4 - k) % 4 * 2 + 1 - core) * rows
            dst = out_ref.at[pl.ds(at, rows), pl.ds(dp_at * cols, cols)]
            arrived(dst, s_send.at[4 * j + k], s_recv.at[4 * j + k])
    own.wait()
    for c in sent:
        c.wait_send()


def gather_tokens(tokens):
    rows, cols = tokens.shape
    dma = pltpu.SemaphoreType.DMA
    return pl.pallas_call(
        gather_kernel,
        out_shape=jax.ShapeDtypeStruct((rows * 8, cols * 4), tokens.dtype),
        in_specs=[pl.BlockSpec(memory_space=pl.ANY)],
        out_specs=pl.BlockSpec(memory_space=pl.ANY),
        scratch_shapes=[dma, dma((3,)), dma((3,))] + [dma((4,))] * 8 + [dma((16,))] * 2,
        compiler_params=pltpu.CompilerParams(collective_id=0, has_side_effects=True, vmem_limit_bytes=VMEM_BYTES),
    )(tokens)


def combine_kernel(hid_ref, down_ref, basis_ref, w_ref, out_ref, zfull_ref, sbuf, rbuf, pbuf, dxb, dyb, xb, yb, zb, zr, zs, zn, z2, zz,
                   s_send, s_recv, dx_send, dx_recv, dy_send, dy_recv, x_send, x_recv, y_send, y_recv, z_send, z_recv, q_send, q_recv):
    dp, expert, y, x, z, core = place()
    rows, cols = out_ref.shape
    half = rows // 2
    x_dp, y_dp, d_dp = y * 2 + 1 - x, (1 - y) * 2 + x, (1 - y) * 2 + 1 - x
    targets = (dp, x_dp, y_dp, d_dp)
    other = (dp, z * 2 + 1 - core)
    x_dev, y_dev = (x_dp, expert), (y_dp, expert)
    z_devs = [(dp, (z + k) % 4 * 2 + core) for k in range(1, 4)]
    enter([other, x_dev, y_dev] + z_devs)

    def copy(ref, dst, send, recv, device):
        return pltpu.make_async_remote_copy(
            src_ref=ref, dst_ref=dst, send_sem=send, recv_sem=recv, device_id=device, device_id_type=MESH
        )

    def q_copy(i, ref, dst, device):
        return copy(ref, dst, q_send.at[i], q_recv.at[i], device)

    count = zs.shape[0] // 2
    lo, hi = pl.ds(0, count), pl.ds(count, count)
    zs[...] = jnp.dot(hid_ref[...], basis_ref[...], preferred_element_type=jnp.float32).astype(zs.dtype)
    q = [
        q_copy(0, zs.at[lo], zn.at[lo], x_dev),
        q_copy(1, zs.at[hi], zn.at[hi], y_dev),
        q_copy(2, z2.at[lo], zz.at[lo], y_dev),
        q_copy(3, z2.at[hi], zz.at[hi], x_dev),
    ]
    q[0].start()
    q[1].start()

    def product(k, j, side):
        at = pl.multiple_of(((z + k) % 4 * 2 + side) * rows, rows)
        col = pl.multiple_of(targets[j] * cols, cols)
        dot = jnp.dot(hid_ref[pl.ds(at, rows), :], down_ref[:, pl.ds(col, cols)], preferred_element_type=jnp.float32)
        return dot * w_ref[pl.ds(at, rows), :]

    def s_copy(k, j):
        return copy(sbuf.at[k, j], rbuf.at[k, j], s_send.at[k, j], s_recv.at[k, j], other)

    def dx_copy(k):
        return copy(pbuf.at[k, 3, pl.ds(0, half)], dxb.at[k], dx_send.at[k], dx_recv.at[k], x_dev)

    def dy_copy(k):
        return copy(pbuf.at[k, 3, pl.ds(half, half)], dyb.at[k], dy_send.at[k], dy_recv.at[k], y_dev)

    def x_copy(k):
        return copy(pbuf.at[k, 1], xb.at[k], x_send.at[k], x_recv.at[k], x_dev)

    def y_copy(k):
        return copy(pbuf.at[k, 2], yb.at[k], y_send.at[k], y_recv.at[k], y_dev)

    def z_copy(k):
        return copy(zb.at[k - 1], zr.at[k - 1], z_send.at[k - 1], z_recv.at[k - 1], z_devs[k - 1])

    order = (2, 1, 3, 0)
    for k in order:
        for j in (3, 1, 2, 0):
            sbuf[k, j] = product(k, j, 1 - core).astype(sbuf.dtype)
            s_copy(k, j).start()
    for i, part in ((0, lo), (1, hi)):
        q[i].wait_recv()
        z2[part, :] = (zs[part, :].astype(jnp.float32) + zn[part, :].astype(jnp.float32)).astype(z2.dtype)
        q[2 + i].start()

    def own(k, j):
        mine = product(k, j, core)
        s_copy(k, j).wait_recv()
        pbuf[k, j] = (mine + rbuf[k, j].astype(jnp.float32)).astype(pbuf.dtype)

    def first(k):
        own(k, 3)
        dx_copy(k).start()
        dy_copy(k).start()
        own(k, 1)
        own(k, 2)
        own(k, 0)

    def second(k):
        dx_copy(k).wait_recv()
        pbuf[k, 2, 0:half] = (pbuf[k, 2, 0:half].astype(jnp.float32) + dxb[k].astype(jnp.float32)).astype(pbuf.dtype)
        y_copy(k).start()
        dy_copy(k).wait_recv()
        pbuf[k, 1, half:rows] = (pbuf[k, 1, half:rows].astype(jnp.float32) + dyb[k].astype(jnp.float32)).astype(pbuf.dtype)
        x_copy(k).start()

    def third(k):
        x_copy(k).wait_recv()
        y_copy(k).wait_recv()
        return pbuf[k, 0].astype(jnp.float32) + xb[k].astype(jnp.float32) + yb[k].astype(jnp.float32)

    def fourth(k):
        zb[k - 1] = third(k).astype(zb.dtype)
        z_copy(k).start()

    for k in order:
        first(k)
    q[2].wait_recv()
    q[3].wait_recv()
    zfull_ref[...] = (z2[...].astype(jnp.float32) + zz[...].astype(jnp.float32)).astype(zfull_ref.dtype)
    second(2)
    second(1)
    second(3)
    fourth(2)
    second(0)
    fourth(1)
    fourth(3)
    total = third(0)
    for k in (2, 1, 3):
        z_copy(k).wait_recv()
        total = total + zr[k - 1].astype(jnp.float32)
    out_ref[...] = total.astype(out_ref.dtype)
    for c in q:
        c.wait_send()
    for k in range(4):
        for j in range(4):
            s_copy(k, j).wait_send()
        for c in (dx_copy, dy_copy, x_copy, y_copy):
            c(k).wait_send()
        if k:
            z_copy(k).wait_send()


def combine(hidden, down, basis, weight, rows, cols):
    total, sk = hidden.shape[0], basis.shape[1]
    dma, vmem, kind = pltpu.SemaphoreType.DMA, pltpu.VMEM, jnp.bfloat16
    spec = pl.BlockSpec(memory_space=pltpu.VMEM)
    return pl.pallas_call(
        combine_kernel,
        out_shape=(jax.ShapeDtypeStruct((rows, cols), kind), jax.ShapeDtypeStruct((total, sk), kind)),
        in_specs=[spec] * 4,
        out_specs=(spec, spec),
        scratch_shapes=[vmem((4, 4, rows, cols), kind)] * 3
        + [vmem((4, rows // 2, cols), kind)] * 2
        + [vmem((4, rows, cols), kind)] * 2
        + [vmem((3, rows, cols), kind)] * 2
        + [vmem((total, sk), kind)] * 4
        + [dma((4, 4))] * 2
        + [dma((4,))] * 8
        + [dma((3,))] * 2
        + [dma((4,))] * 2,
        compiler_params=pltpu.CompilerParams(collective_id=1, has_side_effects=True, vmem_limit_bytes=VMEM_BYTES),
    )(hidden, down, basis, weight)


def dense_body(tokens, routes, route_weights, gate_weight, up_weight, down_weight, sketch_basis):
    owners = lax.axis_size("expert")
    experts = jnp.arange(owners, dtype=jnp.int32)
    table = jnp.sum(jnp.where(routes[:, :, None] == experts, route_weights[:, :, None], 0.0), axis=1)
    tables = lax.all_gather(table, "expert", axis=0, tiled=True)
    features = gather_tokens(tokens)
    weight = jnp.sum(jnp.where(experts == lax.axis_index("expert"), tables, 0.0), axis=1, keepdims=True)
    gate_val = jnp.dot(features, gate_weight[0], preferred_element_type=jnp.float32)
    up_val = jnp.dot(features, up_weight[0], preferred_element_type=jnp.float32)
    hidden = jnp.where(weight > 0, jax.nn.silu(gate_val) * up_val, 0.0).astype(jnp.bfloat16)
    mixed, sketch_full = combine(hidden, down_weight[0], sketch_basis, weight, *tokens.shape)
    contract = (((0,), (0,)), ((), ()))
    gram = lax.dot_general(sketch_full, sketch_full, contract, preferred_element_type=jnp.float32)
    lower_factor = jnp.linalg.cholesky(gram + ridge_term * jnp.eye(gram.shape[0], dtype=jnp.float32))
    projected = lax.dot_general(sketch_full, hidden, contract, preferred_element_type=jnp.float32)
    whitened = jax.scipy.linalg.solve_triangular(lower_factor, projected, lower=True)
    return (mixed, whitened[None])


def solution(mesh):
    dense = mesh.shape["dp"] == 4 and mesh.shape["expert"] == 8
    return jax.shard_map(
        dense_body if dense else body,
        mesh=mesh,
        in_specs=(
            P("expert", "dp"),
            P("expert", None),
            P("expert", None),
            P("expert", None, "dp"),
            P("expert", None, "dp"),
            P("expert", "dp", None),
            P("dp", None),
        ),
        out_specs=(P("expert", "dp"), P("expert", None, "dp")),
        check_vma=False,
    )
```

```python
import jax
import jax.numpy as jnp
from jax import lax
from jax.experimental import pallas as pl
from jax.experimental.pallas import tpu as pltpu
from jax.sharding import PartitionSpec as P

MESH = pl.DeviceIdType.MESH
VMEM_BYTES = 56 * 1024 * 1024

ridge_term = 1.0


def gram_matrix(factor_rows):
    return jnp.dot(factor_rows.T, factor_rows, precision=lax.Precision.HIGHEST)


def body(tokens, routes, route_weights, gate_weight, up_weight, down_weight, sketch_basis):
    owners = lax.axis_size("expert")
    token_count, route_count = routes.shape
    pair_count = token_count * route_count
    capacity = 2 * pair_count // owners
    slot_total = owners * capacity
    route_list = routes.reshape(-1)
    onehot = (route_list[:, None] == jnp.arange(owners, dtype=jnp.int32)[None, :]).astype(jnp.int32)
    before = jnp.cumsum(onehot, axis=0) - onehot
    slot_of = jnp.sum(before * onehot, axis=1)
    counts = jnp.sum(onehot, axis=0)
    target = route_list * capacity + slot_of
    source_pair = (
        jnp.zeros((slot_total,), jnp.int32).at[target].set(jnp.arange(pair_count, dtype=jnp.int32))
    )
    source_token = source_pair // route_count
    count_wire = counts.astype(jnp.bfloat16)
    features = lax.all_gather(tokens, "dp", axis=1, tiled=True)
    outgoing = features[source_token].reshape(owners, capacity, features.shape[1])
    arrived, arrived_counts = (
        lax.all_to_all(outgoing, "expert", split_axis=0, concat_axis=0, tiled=True),
        lax.all_to_all(count_wire, "expert", split_axis=0, concat_axis=0, tiled=True),
    )
    width = arrived.shape[2]
    live_count = arrived_counts.astype(jnp.int32)
    live_mask = (jnp.arange(capacity, dtype=jnp.int32)[None, :] < live_count[:, None]).reshape(-1)
    slot_rows = jnp.where(
        live_mask[:, None], arrived.reshape(slot_total, width), jnp.zeros((), jnp.bfloat16)
    )
    gate_local = gate_weight[0]
    up_local = up_weight[0]
    down_local = down_weight[0]
    gate_val = jnp.dot(slot_rows, gate_local, preferred_element_type=jnp.float32)
    up_val = jnp.dot(slot_rows, up_local, preferred_element_type=jnp.float32)
    hidden_block = (jax.nn.silu(gate_val) * up_val).astype(jnp.bfloat16)
    partial_value = jnp.dot(hidden_block, down_local, preferred_element_type=jnp.float32)
    sums = lax.psum_scatter(
        partial_value.reshape(owners, capacity, width).astype(jnp.bfloat16),
        "dp",
        scatter_dimension=2,
        tiled=True,
    )
    returned = lax.all_to_all(sums, "expert", split_axis=0, concat_axis=0, tiled=True)
    picked = returned.reshape(slot_total, returned.shape[2])[target]
    weighted = jnp.einsum(
        "tkd,tk->td",
        picked.reshape(token_count, route_count, returned.shape[2]).astype(jnp.float32),
        route_weights,
    )
    mixed = weighted.astype(jnp.bfloat16)
    sketch_part = jnp.dot(hidden_block, sketch_basis, preferred_element_type=jnp.float32)
    sketch_width = sketch_part.shape[1]
    eye_matrix = jnp.eye(sketch_width, dtype=jnp.float32)
    sketch_full = lax.psum(sketch_part.astype(jnp.bfloat16), "dp").astype(jnp.float32)
    lower_factor = jnp.linalg.cholesky(gram_matrix(sketch_full) + ridge_term * eye_matrix)
    projected = jnp.dot(
        sketch_full.T, hidden_block.astype(jnp.float32), precision=lax.Precision.HIGHEST
    )
    whitened = jax.scipy.linalg.solve_triangular(lower_factor, projected, lower=True)
    return (mixed, whitened[None])


def place():
    dp, expert = lax.axis_index("dp"), lax.axis_index("expert")
    y, x = dp // 2, dp % 2
    z, core = expert // 2, expert % 2
    return dp, expert, y, x, z, core


def enter(partners):
    barrier = pltpu.get_barrier_semaphore()
    for partner in partners:
        pl.semaphore_signal(barrier, inc=1, device_id=partner, device_id_type=MESH)
    pl.semaphore_wait(barrier, len(partners))


def gather_kernel(tok_ref, tab_ref, out_ref, tabs_ref, own_sem, tab_sem, t_send, t_recv, z_send, z_recv, x_send, x_recv, y_send, y_recv, dx_send, dx_recv, dy_send, dy_recv, s_send, s_recv):
    dp, expert, y, x, z, core = place()
    rows, cols = tok_ref.shape
    half = rows // 2
    x_dp, y_dp, d_dp = y * 2 + 1 - x, (1 - y) * 2 + x, (1 - y) * 2 + 1 - x
    other = (dp, z * 2 + 1 - core)
    x_dev, y_dev = (x_dp, expert), (y_dp, expert)
    z_devs = [(dp, (z + k) % 4 * 2 + core) for k in range(1, 4)]
    cross = [(dp, (z + k) % 4 * 2 + 1 - core) for k in range(1, 4)]
    enter([other, x_dev, y_dev] + z_devs + cross)

    def block(dp_at, k, low=0, count=rows):
        at = ((z + 4 - k) % 4 * 2 + core) * rows + low
        return out_ref.at[pl.ds(at, count), pl.ds(dp_at * cols, cols)]

    def copy(ref, dst, send, recv, device):
        return pltpu.make_async_remote_copy(
            src_ref=ref, dst_ref=dst, send_sem=send, recv_sem=recv, device_id=device, device_id_type=MESH
        )

    sent = []

    def go(*args):
        c = copy(*args)
        c.start()
        sent.append(c)

    def arrived(dst, send, recv):
        copy(dst, dst, send, recv, other).wait_recv()

    own = pltpu.make_async_copy(tok_ref, block(dp, 0), own_sem)
    own.start()

    def table_at(k, side):
        return tabs_ref.at[pl.ds(((z + 4 - k) % 4 * 2 + side) * rows, rows), :]

    own_tab = pltpu.make_async_copy(tab_ref, table_at(0, core), tab_sem)
    own_tab.start()
    go(tok_ref, block(dp, 0), x_send.at[0], x_recv.at[0], x_dev)
    go(tok_ref, block(dp, 0), y_send.at[0], y_recv.at[0], y_dev)
    for k in range(1, 4):
        go(tok_ref, block(dp, 0), z_send.at[k - 1], z_recv.at[k - 1], z_devs[k - 1])
    go(tok_ref, block(dp, 0), s_send.at[0], s_recv.at[0], other)
    for i, device in enumerate([other] + z_devs + cross):
        go(tab_ref, table_at(0, core), t_send.at[i], t_recv.at[i], device)

    def near(k):
        arrived(block(x_dp, k), x_send.at[k], x_recv.at[k])
        go(block(x_dp, k, 0, half), block(x_dp, k, 0, half), dy_send.at[k], dy_recv.at[k], y_dev)
        go(block(x_dp, k), block(x_dp, k), s_send.at[4 + k], s_recv.at[4 + k], other)
        arrived(block(y_dp, k), y_send.at[k], y_recv.at[k])
        go(block(y_dp, k, half, half), block(y_dp, k, half, half), dx_send.at[k], dx_recv.at[k], x_dev)
        go(block(y_dp, k), block(y_dp, k), s_send.at[8 + k], s_recv.at[8 + k], other)

    def far(k):
        arrived(block(d_dp, k, 0, half), dy_send.at[k], dy_recv.at[k])
        arrived(block(d_dp, k, half, half), dx_send.at[k], dx_recv.at[k])
        go(block(d_dp, k), block(d_dp, k), s_send.at[12 + k], s_recv.at[12 + k], other)

    def column(k):
        arrived(block(dp, k), z_send.at[k - 1], z_recv.at[k - 1])
        go(block(dp, k), block(dp, k), x_send.at[k], x_recv.at[k], x_dev)
        go(block(dp, k), block(dp, k), y_send.at[k], y_recv.at[k], y_dev)
        go(block(dp, k), block(dp, k), s_send.at[k], s_recv.at[k], other)

    column(1)
    near(0)
    column(3)
    column(2)
    near(1)
    far(0)
    near(3)
    far(1)
    near(2)
    far(3)
    far(2)
    for j, dp_at in enumerate((dp, x_dp, y_dp, d_dp)):
        for k in range(4):
            at = ((z + 4 - k) % 4 * 2 + 1 - core) * rows
            dst = out_ref.at[pl.ds(at, rows), pl.ds(dp_at * cols, cols)]
            arrived(dst, s_send.at[4 * j + k], s_recv.at[4 * j + k])
    for i in range(7):
        k, side = (0, 1 - core) if i == 0 else (i, core) if i < 4 else (i - 3, 1 - core)
        arrived(table_at(k, side), t_send.at[i], t_recv.at[i])
    own.wait()
    own_tab.wait()
    for c in sent:
        c.wait_send()


def gather_tokens(tokens, table):
    rows, cols = tokens.shape
    dma = pltpu.SemaphoreType.DMA
    return pl.pallas_call(
        gather_kernel,
        out_shape=(
            jax.ShapeDtypeStruct((rows * 8, cols * 4), tokens.dtype),
            jax.ShapeDtypeStruct((rows * 8, table.shape[1]), table.dtype),
        ),
        in_specs=[pl.BlockSpec(memory_space=pl.ANY)] * 2,
        out_specs=(pl.BlockSpec(memory_space=pl.ANY),) * 2,
        scratch_shapes=[dma, dma, dma((7,)), dma((7,)), dma((3,)), dma((3,))] + [dma((4,))] * 8 + [dma((16,))] * 2,
        compiler_params=pltpu.CompilerParams(collective_id=0, has_side_effects=True, vmem_limit_bytes=VMEM_BYTES),
    )(tokens, table)


def combine_kernel(hid_ref, down_ref, basis_ref, w_ref, out_ref, sketch_ref, work, sbuf, rbuf, pbuf, dxb, dyb, xb, yb, zb, zr, zs, zn, z2, zz,
                   s_send, s_recv, dx_send, dx_recv, dy_send, dy_recv, x_send, x_recv, y_send, y_recv, z_send, z_recv, q_send, q_recv):
    dp, expert, y, x, z, core = place()
    rows, cols = out_ref.shape
    half = rows // 2
    x_dp, y_dp, d_dp = y * 2 + 1 - x, (1 - y) * 2 + x, (1 - y) * 2 + 1 - x
    targets = (dp, x_dp, y_dp, d_dp)
    other = (dp, z * 2 + 1 - core)
    x_dev, y_dev = (x_dp, expert), (y_dp, expert)
    z_devs = [(dp, (z + k) % 4 * 2 + core) for k in range(1, 4)]
    enter([other, x_dev, y_dev] + z_devs)

    def copy(ref, dst, send, recv, device):
        return pltpu.make_async_remote_copy(
            src_ref=ref, dst_ref=dst, send_sem=send, recv_sem=recv, device_id=device, device_id_type=MESH
        )

    def q_copy(i, ref, dst, device):
        return copy(ref, dst, q_send.at[i], q_recv.at[i], device)

    count = zs.shape[0] // 2
    lo, hi = pl.ds(0, count), pl.ds(count, count)
    zs[...] = jnp.dot(hid_ref[...], basis_ref[...], preferred_element_type=jnp.float32).astype(zs.dtype)
    q = [
        q_copy(0, zs.at[lo], zn.at[lo], x_dev),
        q_copy(1, zs.at[hi], zn.at[hi], y_dev),
        q_copy(2, z2.at[lo], zz.at[lo], y_dev),
        q_copy(3, z2.at[hi], zz.at[hi], x_dev),
    ]
    q[0].start()
    q[1].start()

    def product(k, j, side):
        at = pl.multiple_of(((z + k) % 4 * 2 + side) * rows, rows)
        col = pl.multiple_of(targets[j] * cols, cols)
        dot = jnp.dot(hid_ref[pl.ds(at, rows), :], down_ref[:, pl.ds(col, cols)], preferred_element_type=jnp.float32)
        return dot * w_ref[pl.ds(at, rows), :]

    def s_copy(k, j):
        return copy(sbuf.at[k, j], rbuf.at[k, j], s_send.at[k, j], s_recv.at[k, j], other)

    def dx_copy(k):
        return copy(pbuf.at[k, 3, pl.ds(0, half)], dxb.at[k], dx_send.at[k], dx_recv.at[k], x_dev)

    def dy_copy(k):
        return copy(pbuf.at[k, 3, pl.ds(half, half)], dyb.at[k], dy_send.at[k], dy_recv.at[k], y_dev)

    def x_copy(k):
        return copy(pbuf.at[k, 1], xb.at[k], x_send.at[k], x_recv.at[k], x_dev)

    def y_copy(k):
        return copy(pbuf.at[k, 2], yb.at[k], y_send.at[k], y_recv.at[k], y_dev)

    def z_copy(k):
        return copy(zb.at[k - 1], zr.at[k - 1], z_send.at[k - 1], z_recv.at[k - 1], z_devs[k - 1])

    order = (2, 1, 3, 0)
    for k in order:
        for j in (3, 1, 2, 0):
            sbuf[k, j] = product(k, j, 1 - core).astype(sbuf.dtype)
            s_copy(k, j).start()
    for i, part in ((0, lo), (1, hi)):
        q[i].wait_recv()
        z2[part, :] = (zs[part, :].astype(jnp.float32) + zn[part, :].astype(jnp.float32)).astype(z2.dtype)
        q[2 + i].start()

    def own(k, j):
        mine = product(k, j, core)
        s_copy(k, j).wait_recv()
        pbuf[k, j] = (mine + rbuf[k, j].astype(jnp.float32)).astype(pbuf.dtype)

    def first(k):
        own(k, 3)
        dx_copy(k).start()
        dy_copy(k).start()
        own(k, 1)
        own(k, 2)
        own(k, 0)

    def second(k):
        dx_copy(k).wait_recv()
        pbuf[k, 2, 0:half] = (pbuf[k, 2, 0:half].astype(jnp.float32) + dxb[k].astype(jnp.float32)).astype(pbuf.dtype)
        y_copy(k).start()
        dy_copy(k).wait_recv()
        pbuf[k, 1, half:rows] = (pbuf[k, 1, half:rows].astype(jnp.float32) + dyb[k].astype(jnp.float32)).astype(pbuf.dtype)
        x_copy(k).start()

    def third(k):
        x_copy(k).wait_recv()
        y_copy(k).wait_recv()
        return pbuf[k, 0].astype(jnp.float32) + xb[k].astype(jnp.float32) + yb[k].astype(jnp.float32)

    def fourth(k):
        zb[k - 1] = third(k).astype(zb.dtype)
        z_copy(k).start()

    for k in order:
        first(k)
    q[2].wait_recv()
    q[3].wait_recv()
    q[0].wait_send()
    q[1].wait_send()
    zs[...] = (z2[...].astype(jnp.float32) + zz[...].astype(jnp.float32)).astype(zs.dtype)
    second(2)
    second(1)
    second(3)
    second(0)
    sk = work.shape[0]
    panel_rows = 32
    contract = (((0,), (0,)), ((), ()))
    line = lax.broadcasted_iota(jnp.int32, (sk, sk), 0)
    eye = (line == lax.broadcasted_iota(jnp.int32, (sk, sk), 1)).astype(jnp.float32)
    work[:, 0:sk] = lax.dot_general(zs[...], zs[...], contract, preferred_element_type=jnp.float32) + ridge_term * eye
    work[:, sk:] = eye

    def eliminate(p):
        low = p * panel_rows
        lanes = lax.broadcasted_iota(jnp.int32, (panel_rows, 2 * sk), 1)
        lines = lax.broadcasted_iota(jnp.int32, (panel_rows, 2 * sk), 0)

        def step(r, panel):
            row = jnp.sum(jnp.where(lines == r, panel, 0.0), axis=0, keepdims=True)
            column = jnp.sum(jnp.where(lanes[:, :sk] == low + r, panel[:, :sk], 0.0), axis=1, keepdims=True)
            pivot = jnp.sum(jnp.where(lanes[0:1, :sk] == low + r, row[:, :sk], 0.0), axis=1, keepdims=True)
            scale = lax.rsqrt(pivot)
            row = row * scale
            below = panel - (column * scale) * row
            return jnp.where(lines < r, panel, jnp.where(lines == r, row, below))

        panel = lax.fori_loop(0, panel_rows, step, work[low : low + panel_rows, :])
        work[low : low + panel_rows, :] = panel
        high = low + panel_rows
        if high < sk:
            update = lax.dot_general(
                panel[:, :sk], panel, contract, precision=lax.Precision.HIGHEST, preferred_element_type=jnp.float32
            )
            work[high:, :] = work[high:, :] - update[high:, :]

    eliminate(0)
    fourth(2)
    eliminate(1)
    fourth(1)
    eliminate(2)
    fourth(3)
    eliminate(3)
    total = third(0)
    projected = lax.dot_general(zs[...], hid_ref[...], contract, preferred_element_type=jnp.float32)
    sketch_ref[...] = jnp.dot(
        work[:, sk:], projected, precision=lax.Precision.HIGHEST, preferred_element_type=jnp.float32
    )
    for k in (2, 1, 3):
        z_copy(k).wait_recv()
        total = total + zr[k - 1].astype(jnp.float32)
    out_ref[...] = total.astype(out_ref.dtype)
    for c in q[2:]:
        c.wait_send()
    for k in range(4):
        for j in range(4):
            s_copy(k, j).wait_send()
        for c in (dx_copy, dy_copy, x_copy, y_copy):
            c(k).wait_send()
        if k:
            z_copy(k).wait_send()


def combine(hidden, down, basis, weight, rows, cols):
    total, sk = hidden.shape[0], basis.shape[1]
    dma, vmem, kind = pltpu.SemaphoreType.DMA, pltpu.VMEM, jnp.bfloat16
    spec = pl.BlockSpec(memory_space=pltpu.VMEM)
    return pl.pallas_call(
        combine_kernel,
        out_shape=(jax.ShapeDtypeStruct((rows, cols), kind), jax.ShapeDtypeStruct((sk, hidden.shape[1]), jnp.float32)),
        in_specs=[spec] * 4,
        out_specs=(spec, spec),
        scratch_shapes=[vmem((sk, 2 * sk), jnp.float32)]
        + [vmem((4, 4, rows, cols), kind)] * 3
        + [vmem((4, rows // 2, cols), kind)] * 2
        + [vmem((4, rows, cols), kind)] * 2
        + [vmem((3, rows, cols), kind)] * 2
        + [vmem((total, sk), kind)] * 4
        + [dma((4, 4))] * 2
        + [dma((4,))] * 8
        + [dma((3,))] * 2
        + [dma((4,))] * 2,
        compiler_params=pltpu.CompilerParams(collective_id=1, has_side_effects=True, vmem_limit_bytes=VMEM_BYTES),
    )(hidden, down, basis, weight)


def dense_body(tokens, routes, route_weights, gate_weight, up_weight, down_weight, sketch_basis):
    owners = lax.axis_size("expert")
    experts = jnp.arange(owners, dtype=jnp.int32)
    table = jnp.sum(jnp.where(routes[:, :, None] == experts, route_weights[:, :, None], 0.0), axis=1)
    features, tables = gather_tokens(tokens, table)
    weight = jnp.sum(jnp.where(experts == lax.axis_index("expert"), tables, 0.0), axis=1, keepdims=True)
    gate_val = jnp.dot(features, gate_weight[0], preferred_element_type=jnp.float32)
    up_val = jnp.dot(features, up_weight[0], preferred_element_type=jnp.float32)
    hidden = jnp.where(weight > 0, jax.nn.silu(gate_val) * up_val, 0.0).astype(jnp.bfloat16)
    mixed, whitened = combine(hidden, down_weight[0], sketch_basis, weight, *tokens.shape)
    return (mixed, whitened[None])


def solution(mesh):
    dense = mesh.shape["dp"] == 4 and mesh.shape["expert"] == 8
    return jax.shard_map(
        dense_body if dense else body,
        mesh=mesh,
        in_specs=(
            P("expert", "dp"),
            P("expert", None),
            P("expert", None),
            P("expert", None, "dp"),
            P("expert", None, "dp"),
            P("expert", "dp", None),
            P("dp", None),
        ),
        out_specs=(P("expert", "dp"), P("expert", None, "dp")),
        check_vma=False,
    )
```

```python
import jax
import jax.numpy as jnp
from jax import lax
from jax.experimental import pallas as pl
from jax.experimental.pallas import tpu as pltpu
from jax.sharding import PartitionSpec as P

MESH = pl.DeviceIdType.MESH
VMEM_BYTES = 56 * 1024 * 1024

ridge_term = 1.0


def gram_matrix(factor_rows):
    return jnp.dot(factor_rows.T, factor_rows, precision=lax.Precision.HIGHEST)


def body(tokens, routes, route_weights, gate_weight, up_weight, down_weight, sketch_basis):
    owners = lax.axis_size("expert")
    token_count, route_count = routes.shape
    pair_count = token_count * route_count
    capacity = 2 * pair_count // owners
    slot_total = owners * capacity
    route_list = routes.reshape(-1)
    onehot = (route_list[:, None] == jnp.arange(owners, dtype=jnp.int32)[None, :]).astype(jnp.int32)
    before = jnp.cumsum(onehot, axis=0) - onehot
    slot_of = jnp.sum(before * onehot, axis=1)
    counts = jnp.sum(onehot, axis=0)
    target = route_list * capacity + slot_of
    source_pair = (
        jnp.zeros((slot_total,), jnp.int32).at[target].set(jnp.arange(pair_count, dtype=jnp.int32))
    )
    source_token = source_pair // route_count
    count_wire = counts.astype(jnp.bfloat16)
    features = lax.all_gather(tokens, "dp", axis=1, tiled=True)
    outgoing = features[source_token].reshape(owners, capacity, features.shape[1])
    arrived, arrived_counts = (
        lax.all_to_all(outgoing, "expert", split_axis=0, concat_axis=0, tiled=True),
        lax.all_to_all(count_wire, "expert", split_axis=0, concat_axis=0, tiled=True),
    )
    width = arrived.shape[2]
    live_count = arrived_counts.astype(jnp.int32)
    live_mask = (jnp.arange(capacity, dtype=jnp.int32)[None, :] < live_count[:, None]).reshape(-1)
    slot_rows = jnp.where(
        live_mask[:, None], arrived.reshape(slot_total, width), jnp.zeros((), jnp.bfloat16)
    )
    gate_local = gate_weight[0]
    up_local = up_weight[0]
    down_local = down_weight[0]
    gate_val = jnp.dot(slot_rows, gate_local, preferred_element_type=jnp.float32)
    up_val = jnp.dot(slot_rows, up_local, preferred_element_type=jnp.float32)
    hidden_block = (jax.nn.silu(gate_val) * up_val).astype(jnp.bfloat16)
    partial_value = jnp.dot(hidden_block, down_local, preferred_element_type=jnp.float32)
    sums = lax.psum_scatter(
        partial_value.reshape(owners, capacity, width).astype(jnp.bfloat16),
        "dp",
        scatter_dimension=2,
        tiled=True,
    )
    returned = lax.all_to_all(sums, "expert", split_axis=0, concat_axis=0, tiled=True)
    picked = returned.reshape(slot_total, returned.shape[2])[target]
    weighted = jnp.einsum(
        "tkd,tk->td",
        picked.reshape(token_count, route_count, returned.shape[2]).astype(jnp.float32),
        route_weights,
    )
    mixed = weighted.astype(jnp.bfloat16)
    sketch_part = jnp.dot(hidden_block, sketch_basis, preferred_element_type=jnp.float32)
    sketch_width = sketch_part.shape[1]
    eye_matrix = jnp.eye(sketch_width, dtype=jnp.float32)
    sketch_full = lax.psum(sketch_part.astype(jnp.bfloat16), "dp").astype(jnp.float32)
    lower_factor = jnp.linalg.cholesky(gram_matrix(sketch_full) + ridge_term * eye_matrix)
    projected = jnp.dot(
        sketch_full.T, hidden_block.astype(jnp.float32), precision=lax.Precision.HIGHEST
    )
    whitened = jax.scipy.linalg.solve_triangular(lower_factor, projected, lower=True)
    return (mixed, whitened[None])


def place():
    dp, expert = lax.axis_index("dp"), lax.axis_index("expert")
    y, x = dp // 2, dp % 2
    z, core = expert // 2, expert % 2
    return dp, expert, y, x, z, core


def enter(partners):
    barrier = pltpu.get_barrier_semaphore()
    for partner in partners:
        pl.semaphore_signal(barrier, inc=1, device_id=partner, device_id_type=MESH)
    pl.semaphore_wait(barrier, len(partners))


def hidden_kernel(tok_ref, tab_ref, gate_ref, up_ref, hid_ref, w_ref, out_ref, tabs_ref, gate_w, up_w, gate_acc, up_acc, gw_sem, uw_sem, own_sem, tab_sem, t_send, t_recv, z_send, z_recv, x_send, x_recv, y_send, y_recv, dx_send, dx_recv, dy_send, dy_recv, s_send, s_recv):
    dp, expert, y, x, z, core = place()
    rows, cols = tok_ref.shape
    half = rows // 2
    x_dp, y_dp, d_dp = y * 2 + 1 - x, (1 - y) * 2 + x, (1 - y) * 2 + 1 - x
    other = (dp, z * 2 + 1 - core)
    x_dev, y_dev = (x_dp, expert), (y_dp, expert)
    z_devs = [(dp, (z + k) % 4 * 2 + core) for k in range(1, 4)]
    cross = [(dp, (z + k) % 4 * 2 + 1 - core) for k in range(1, 4)]
    enter([other, x_dev, y_dev] + z_devs + cross)

    def block(dp_at, k, low=0, count=rows):
        at = ((z + 4 - k) % 4 * 2 + core) * rows + low
        return out_ref.at[pl.ds(at, count), pl.ds(dp_at * cols, cols)]

    def copy(ref, dst, send, recv, device):
        return pltpu.make_async_remote_copy(
            src_ref=ref, dst_ref=dst, send_sem=send, recv_sem=recv, device_id=device, device_id_type=MESH
        )

    weights = (pltpu.make_async_copy(gate_ref, gate_w, gw_sem), pltpu.make_async_copy(up_ref, up_w, uw_sem))
    sent = []

    def go(*args):
        c = copy(*args)
        c.start()
        sent.append(c)

    def arrived(dst, send, recv):
        copy(dst, dst, send, recv, other).wait_recv()

    own = pltpu.make_async_copy(tok_ref, block(dp, 0), own_sem)
    own.start()

    def table_at(k, side):
        return tabs_ref.at[pl.ds(((z + 4 - k) % 4 * 2 + side) * rows, rows), :]

    own_tab = pltpu.make_async_copy(tab_ref, table_at(0, core), tab_sem)
    own_tab.start()
    go(tok_ref, block(dp, 0), x_send.at[0], x_recv.at[0], x_dev)
    go(tok_ref, block(dp, 0), y_send.at[0], y_recv.at[0], y_dev)
    for k in range(1, 4):
        go(tok_ref, block(dp, 0), z_send.at[k - 1], z_recv.at[k - 1], z_devs[k - 1])
    go(tok_ref, block(dp, 0), s_send.at[0], s_recv.at[0], other)
    for i, device in enumerate([other] + z_devs + cross):
        go(tab_ref, table_at(0, core), t_send.at[i], t_recv.at[i], device)

    def near(k):
        arrived(block(x_dp, k), x_send.at[k], x_recv.at[k])
        go(block(x_dp, k, 0, half), block(x_dp, k, 0, half), dy_send.at[k], dy_recv.at[k], y_dev)
        go(block(x_dp, k), block(x_dp, k), s_send.at[4 + k], s_recv.at[4 + k], other)
        arrived(block(y_dp, k), y_send.at[k], y_recv.at[k])
        go(block(y_dp, k, half, half), block(y_dp, k, half, half), dx_send.at[k], dx_recv.at[k], x_dev)
        go(block(y_dp, k), block(y_dp, k), s_send.at[8 + k], s_recv.at[8 + k], other)

    def far(k):
        arrived(block(d_dp, k, 0, half), dy_send.at[k], dy_recv.at[k])
        arrived(block(d_dp, k, half, half), dx_send.at[k], dx_recv.at[k])
        go(block(d_dp, k), block(d_dp, k), s_send.at[12 + k], s_recv.at[12 + k], other)

    def column(k):
        arrived(block(dp, k), z_send.at[k - 1], z_recv.at[k - 1])
        go(block(dp, k), block(dp, k), x_send.at[k], x_recv.at[k], x_dev)
        go(block(dp, k), block(dp, k), y_send.at[k], y_recv.at[k], y_dev)
        go(block(dp, k), block(dp, k), s_send.at[k], s_recv.at[k], other)

    for c in weights:
        c.start()
    columns_of = (dp, x_dp, y_dp, d_dp)

    def pair(j, k):
        at = ((z + 4 - k) % 4 * 2 + 1 - core) * rows
        col = pl.multiple_of(columns_of[j] * cols, cols)
        arrived(out_ref.at[pl.ds(at, rows), pl.ds(col, cols)], s_send.at[4 * j + k], s_recv.at[4 * j + k])
        both = pl.ds(pl.multiple_of((z + 4 - k) % 4 * 2 * rows, 2 * rows), 2 * rows)
        piece = out_ref[both, pl.ds(col, cols)]
        for acc, matrix in ((gate_acc, gate_w), (up_acc, up_w)):
            value = jnp.dot(piece, matrix[pl.ds(col, cols), :], preferred_element_type=jnp.float32)
            acc[both, :] = value if j == 0 else acc[both, :] + value

    def finish(k):
        both = pl.ds(pl.multiple_of((z + 4 - k) % 4 * 2 * rows, 2 * rows), 2 * rows)
        gate = gate_acc[both, :]
        value = gate / (1.0 + jnp.exp(-gate)) * up_acc[both, :]
        hid_ref[both, :] = jnp.where(w_ref[both, :] > 0, value, 0.0).astype(hid_ref.dtype)

    column(1)
    near(0)
    column(3)
    own.wait()
    for c in weights:
        c.wait()
    pair(0, 0)
    column(2)
    pair(1, 0)
    pair(2, 0)
    pair(0, 1)
    near(1)
    far(0)
    own_tab.wait()
    for i in range(7):
        k, side = (0, 1 - core) if i == 0 else (i, core) if i < 4 else (i - 3, 1 - core)
        arrived(table_at(k, side), t_send.at[i], t_recv.at[i])
    experts = lax.broadcasted_iota(jnp.int32, tabs_ref.shape, 1)
    w_ref[...] = jnp.sum(jnp.where(experts == expert, tabs_ref[...], 0.0), axis=1, keepdims=True)
    pair(0, 3)
    pair(0, 2)
    near(3)
    far(1)
    pair(3, 0)
    finish(0)
    pair(1, 1)
    pair(2, 1)
    near(2)
    far(3)
    pair(3, 1)
    finish(1)
    pair(1, 3)
    pair(2, 3)
    far(2)
    pair(3, 3)
    finish(3)
    pair(1, 2)
    pair(2, 2)
    pair(3, 2)
    finish(2)
    for c in sent:
        c.wait_send()


def hidden_units(tokens, table, gate, up):
    rows, cols = tokens.shape
    dma, vmem = pltpu.SemaphoreType.DMA, pltpu.VMEM
    units = gate.shape[1]
    return pl.pallas_call(
        hidden_kernel,
        out_shape=(
            jax.ShapeDtypeStruct((rows * 8, units), tokens.dtype),
            jax.ShapeDtypeStruct((rows * 8, 1), table.dtype),
        ),
        in_specs=[pl.BlockSpec(memory_space=pltpu.VMEM)] * 2 + [pl.BlockSpec(memory_space=pl.ANY)] * 2,
        out_specs=(pl.BlockSpec(memory_space=pltpu.VMEM),) * 2,
        scratch_shapes=[
            vmem((rows * 8, cols * 4), tokens.dtype),
            vmem((rows * 8, table.shape[1]), table.dtype),
            vmem(gate.shape, gate.dtype),
            vmem(up.shape, up.dtype),
            vmem((rows * 8, units), jnp.float32),
            vmem((rows * 8, units), jnp.float32),
        ]
        + [dma] * 4
        + [dma((7,))] * 2
        + [dma((3,))] * 2
        + [dma((4,))] * 8
        + [dma((16,))] * 2,
        compiler_params=pltpu.CompilerParams(collective_id=0, has_side_effects=True, vmem_limit_bytes=VMEM_BYTES),
    )(tokens, table, gate, up)


def combine_kernel(hid_ref, down_ref, basis_ref, w_ref, out_ref, sketch_ref, work, sbuf, rbuf, pbuf, dxb, dyb, xb, yb, zb, zr, zs, zn, z2, zz,
                   s_send, s_recv, dx_send, dx_recv, dy_send, dy_recv, x_send, x_recv, y_send, y_recv, z_send, z_recv, q_send, q_recv):
    dp, expert, y, x, z, core = place()
    rows, cols = out_ref.shape
    half = rows // 2
    x_dp, y_dp, d_dp = y * 2 + 1 - x, (1 - y) * 2 + x, (1 - y) * 2 + 1 - x
    targets = (dp, x_dp, y_dp, d_dp)
    other = (dp, z * 2 + 1 - core)
    x_dev, y_dev = (x_dp, expert), (y_dp, expert)
    z_devs = [(dp, (z + k) % 4 * 2 + core) for k in range(1, 4)]
    enter([other, x_dev, y_dev] + z_devs)

    def copy(ref, dst, send, recv, device):
        return pltpu.make_async_remote_copy(
            src_ref=ref, dst_ref=dst, send_sem=send, recv_sem=recv, device_id=device, device_id_type=MESH
        )

    def q_copy(i, ref, dst, device):
        return copy(ref, dst, q_send.at[i], q_recv.at[i], device)

    count = zs.shape[0] // 2
    lo, hi = pl.ds(0, count), pl.ds(count, count)
    zs[...] = jnp.dot(hid_ref[...], basis_ref[...], preferred_element_type=jnp.float32).astype(zs.dtype)
    q = [
        q_copy(0, zs.at[lo], zn.at[lo], x_dev),
        q_copy(1, zs.at[hi], zn.at[hi], y_dev),
        q_copy(2, z2.at[lo], zz.at[lo], y_dev),
        q_copy(3, z2.at[hi], zz.at[hi], x_dev),
    ]
    q[0].start()
    q[1].start()

    def product(k, j, side):
        at = pl.multiple_of(((z + k) % 4 * 2 + side) * rows, rows)
        col = pl.multiple_of(targets[j] * cols, cols)
        dot = jnp.dot(hid_ref[pl.ds(at, rows), :], down_ref[:, pl.ds(col, cols)], preferred_element_type=jnp.float32)
        return dot * w_ref[pl.ds(at, rows), :]

    def s_copy(k, j):
        return copy(sbuf.at[k, j], rbuf.at[k, j], s_send.at[k, j], s_recv.at[k, j], other)

    def dx_copy(k):
        return copy(pbuf.at[k, 3, pl.ds(0, half)], dxb.at[k], dx_send.at[k], dx_recv.at[k], x_dev)

    def dy_copy(k):
        return copy(pbuf.at[k, 3, pl.ds(half, half)], dyb.at[k], dy_send.at[k], dy_recv.at[k], y_dev)

    def x_copy(k):
        return copy(pbuf.at[k, 1], xb.at[k], x_send.at[k], x_recv.at[k], x_dev)

    def y_copy(k):
        return copy(pbuf.at[k, 2], yb.at[k], y_send.at[k], y_recv.at[k], y_dev)

    def z_copy(k):
        return copy(zb.at[k - 1], zr.at[k - 1], z_send.at[k - 1], z_recv.at[k - 1], z_devs[k - 1])

    order = (2, 1, 3, 0)

    def give(k, j):
        sbuf[k, j] = product(k, j, 1 - core).astype(sbuf.dtype)
        s_copy(k, j).start()

    def own(k, j):
        mine = product(k, j, core)
        s_copy(k, j).wait_recv()
        pbuf[k, j] = (mine + rbuf[k, j].astype(jnp.float32)).astype(pbuf.dtype)

    for k in order:
        give(k, 3)
    for k in order:
        own(k, 3)
        dx_copy(k).start()
        dy_copy(k).start()
    for k in order:
        give(k, 2)
        give(k, 1)
    for i, part in ((0, lo), (1, hi)):
        q[i].wait_recv()
        z2[part, :] = (zs[part, :].astype(jnp.float32) + zn[part, :].astype(jnp.float32)).astype(z2.dtype)
        q[2 + i].start()

    def second(k):
        dx_copy(k).wait_recv()
        pbuf[k, 2, 0:half] = (pbuf[k, 2, 0:half].astype(jnp.float32) + dxb[k].astype(jnp.float32)).astype(pbuf.dtype)
        y_copy(k).start()
        dy_copy(k).wait_recv()
        pbuf[k, 1, half:rows] = (pbuf[k, 1, half:rows].astype(jnp.float32) + dyb[k].astype(jnp.float32)).astype(pbuf.dtype)
        x_copy(k).start()

    def third(k):
        x_copy(k).wait_recv()
        y_copy(k).wait_recv()
        return pbuf[k, 0].astype(jnp.float32) + xb[k].astype(jnp.float32) + yb[k].astype(jnp.float32)

    def fourth(k):
        zb[k - 1] = third(k).astype(zb.dtype)
        z_copy(k).start()

    for k in order:
        own(k, 2)
        own(k, 1)
        second(k)
    for k in order:
        give(k, 0)
    for k in order:
        own(k, 0)
    q[2].wait_recv()
    q[3].wait_recv()
    q[0].wait_send()
    q[1].wait_send()
    zs[...] = (z2[...].astype(jnp.float32) + zz[...].astype(jnp.float32)).astype(zs.dtype)
    sk = work.shape[0]
    panel_rows = 32
    contract = (((0,), (0,)), ((), ()))
    line = lax.broadcasted_iota(jnp.int32, (sk, sk), 0)
    eye = (line == lax.broadcasted_iota(jnp.int32, (sk, sk), 1)).astype(jnp.float32)
    work[:, 0:sk] = lax.dot_general(zs[...], zs[...], contract, preferred_element_type=jnp.float32) + ridge_term * eye
    work[:, sk:] = eye

    def eliminate(p):
        low = p * panel_rows
        lanes = lax.broadcasted_iota(jnp.int32, (panel_rows, 2 * sk), 1)
        lines = lax.broadcasted_iota(jnp.int32, (panel_rows, 2 * sk), 0)

        def step(r, panel):
            row = jnp.sum(jnp.where(lines == r, panel, 0.0), axis=0, keepdims=True)
            column = jnp.sum(jnp.where(lanes[:, :sk] == low + r, panel[:, :sk], 0.0), axis=1, keepdims=True)
            pivot = jnp.sum(jnp.where(lanes[0:1, :sk] == low + r, row[:, :sk], 0.0), axis=1, keepdims=True)
            scale = lax.rsqrt(pivot)
            row = row * scale
            below = panel - (column * scale) * row
            return jnp.where(lines < r, panel, jnp.where(lines == r, row, below))

        panel = lax.fori_loop(0, panel_rows, step, work[low : low + panel_rows, :])
        work[low : low + panel_rows, :] = panel
        high = low + panel_rows
        if high < sk:
            update = lax.dot_general(
                panel[:, :sk], panel, contract, precision=lax.Precision.HIGHEST, preferred_element_type=jnp.float32
            )
            work[high:, :] = work[high:, :] - update[high:, :]

    eliminate(0)
    fourth(2)
    eliminate(1)
    fourth(1)
    eliminate(2)
    fourth(3)
    eliminate(3)
    total = third(0)
    projected = lax.dot_general(zs[...], hid_ref[...], contract, preferred_element_type=jnp.float32)
    sketch_ref[...] = jnp.dot(
        work[:, sk:], projected, precision=lax.Precision.HIGHEST, preferred_element_type=jnp.float32
    )
    for k in (2, 1, 3):
        z_copy(k).wait_recv()
        total = total + zr[k - 1].astype(jnp.float32)
    out_ref[...] = total.astype(out_ref.dtype)
    for c in q[2:]:
        c.wait_send()
    for k in range(4):
        for j in range(4):
            s_copy(k, j).wait_send()
        for c in (dx_copy, dy_copy, x_copy, y_copy):
            c(k).wait_send()
        if k:
            z_copy(k).wait_send()


def combine(hidden, down, basis, weight, rows, cols):
    total, sk = hidden.shape[0], basis.shape[1]
    dma, vmem, kind = pltpu.SemaphoreType.DMA, pltpu.VMEM, jnp.bfloat16
    spec = pl.BlockSpec(memory_space=pltpu.VMEM)
    return pl.pallas_call(
        combine_kernel,
        out_shape=(jax.ShapeDtypeStruct((rows, cols), kind), jax.ShapeDtypeStruct((sk, hidden.shape[1]), jnp.float32)),
        in_specs=[spec] * 4,
        out_specs=(spec, spec),
        scratch_shapes=[vmem((sk, 2 * sk), jnp.float32)]
        + [vmem((4, 4, rows, cols), kind)] * 3
        + [vmem((4, rows // 2, cols), kind)] * 2
        + [vmem((4, rows, cols), kind)] * 2
        + [vmem((3, rows, cols), kind)] * 2
        + [vmem((total, sk), kind)] * 4
        + [dma((4, 4))] * 2
        + [dma((4,))] * 8
        + [dma((3,))] * 2
        + [dma((4,))] * 2,
        compiler_params=pltpu.CompilerParams(collective_id=1, has_side_effects=True, vmem_limit_bytes=VMEM_BYTES),
    )(hidden, down, basis, weight)


def dense_body(tokens, routes, route_weights, gate_weight, up_weight, down_weight, sketch_basis):
    owners = lax.axis_size("expert")
    experts = jnp.arange(owners, dtype=jnp.int32)
    table = jnp.sum(jnp.where(routes[:, :, None] == experts, route_weights[:, :, None], 0.0), axis=1)
    hidden, weight = hidden_units(tokens, table, gate_weight[0], up_weight[0])
    mixed, whitened = combine(hidden, down_weight[0], sketch_basis, weight, *tokens.shape)
    return (mixed, whitened[None])


def solution(mesh):
    dense = mesh.shape["dp"] == 4 and mesh.shape["expert"] == 8
    return jax.shard_map(
        dense_body if dense else body,
        mesh=mesh,
        in_specs=(
            P("expert", "dp"),
            P("expert", None),
            P("expert", None),
            P("expert", None, "dp"),
            P("expert", None, "dp"),
            P("expert", "dp", None),
            P("dp", None),
        ),
        out_specs=(P("expert", "dp"), P("expert", None, "dp")),
        check_vma=False,
    )
```

```python
import jax
import jax.numpy as jnp
from jax import lax
from jax.experimental import pallas as pl
from jax.experimental.pallas import tpu as pltpu
from jax.sharding import PartitionSpec as P

MESH = pl.DeviceIdType.MESH
VMEM_BYTES = 56 * 1024 * 1024

ridge_term = 1.0


def gram_matrix(factor_rows):
    return jnp.dot(factor_rows.T, factor_rows, precision=lax.Precision.HIGHEST)


def body(tokens, routes, route_weights, gate_weight, up_weight, down_weight, sketch_basis):
    owners = lax.axis_size("expert")
    token_count, route_count = routes.shape
    pair_count = token_count * route_count
    capacity = 2 * pair_count // owners
    slot_total = owners * capacity
    route_list = routes.reshape(-1)
    onehot = (route_list[:, None] == jnp.arange(owners, dtype=jnp.int32)[None, :]).astype(jnp.int32)
    before = jnp.cumsum(onehot, axis=0) - onehot
    slot_of = jnp.sum(before * onehot, axis=1)
    counts = jnp.sum(onehot, axis=0)
    target = route_list * capacity + slot_of
    source_pair = (
        jnp.zeros((slot_total,), jnp.int32).at[target].set(jnp.arange(pair_count, dtype=jnp.int32))
    )
    source_token = source_pair // route_count
    count_wire = counts.astype(jnp.bfloat16)
    features = lax.all_gather(tokens, "dp", axis=1, tiled=True)
    outgoing = features[source_token].reshape(owners, capacity, features.shape[1])
    arrived, arrived_counts = (
        lax.all_to_all(outgoing, "expert", split_axis=0, concat_axis=0, tiled=True),
        lax.all_to_all(count_wire, "expert", split_axis=0, concat_axis=0, tiled=True),
    )
    width = arrived.shape[2]
    live_count = arrived_counts.astype(jnp.int32)
    live_mask = (jnp.arange(capacity, dtype=jnp.int32)[None, :] < live_count[:, None]).reshape(-1)
    slot_rows = jnp.where(
        live_mask[:, None], arrived.reshape(slot_total, width), jnp.zeros((), jnp.bfloat16)
    )
    gate_local = gate_weight[0]
    up_local = up_weight[0]
    down_local = down_weight[0]
    gate_val = jnp.dot(slot_rows, gate_local, preferred_element_type=jnp.float32)
    up_val = jnp.dot(slot_rows, up_local, preferred_element_type=jnp.float32)
    hidden_block = (jax.nn.silu(gate_val) * up_val).astype(jnp.bfloat16)
    partial_value = jnp.dot(hidden_block, down_local, preferred_element_type=jnp.float32)
    sums = lax.psum_scatter(
        partial_value.reshape(owners, capacity, width).astype(jnp.bfloat16),
        "dp",
        scatter_dimension=2,
        tiled=True,
    )
    returned = lax.all_to_all(sums, "expert", split_axis=0, concat_axis=0, tiled=True)
    picked = returned.reshape(slot_total, returned.shape[2])[target]
    weighted = jnp.einsum(
        "tkd,tk->td",
        picked.reshape(token_count, route_count, returned.shape[2]).astype(jnp.float32),
        route_weights,
    )
    mixed = weighted.astype(jnp.bfloat16)
    sketch_part = jnp.dot(hidden_block, sketch_basis, preferred_element_type=jnp.float32)
    sketch_width = sketch_part.shape[1]
    eye_matrix = jnp.eye(sketch_width, dtype=jnp.float32)
    sketch_full = lax.psum(sketch_part.astype(jnp.bfloat16), "dp").astype(jnp.float32)
    lower_factor = jnp.linalg.cholesky(gram_matrix(sketch_full) + ridge_term * eye_matrix)
    projected = jnp.dot(
        sketch_full.T, hidden_block.astype(jnp.float32), precision=lax.Precision.HIGHEST
    )
    whitened = jax.scipy.linalg.solve_triangular(lower_factor, projected, lower=True)
    return (mixed, whitened[None])


def place():
    dp, expert = lax.axis_index("dp"), lax.axis_index("expert")
    y, x = dp // 2, dp % 2
    z, core = expert // 2, expert % 2
    return dp, expert, y, x, z, core


def enter(partners):
    barrier = pltpu.get_barrier_semaphore()
    for partner in partners:
        pl.semaphore_signal(barrier, inc=1, device_id=partner, device_id_type=MESH)
    pl.semaphore_wait(barrier, len(partners))


def hidden_kernel(tok_ref, tab_ref, gate_ref, up_ref, hid_ref, w_ref, out_ref, tabs_ref, gate_w, up_w, gate_acc, up_acc, gw_sem, uw_sem, own_sem, tab_sem, t_send, t_recv, z_send, z_recv, x_send, x_recv, y_send, y_recv, dx_send, dx_recv, dy_send, dy_recv, s_send, s_recv):
    dp, expert, y, x, z, core = place()
    rows, cols = tok_ref.shape
    half = rows // 2
    x_dp, y_dp, d_dp = y * 2 + 1 - x, (1 - y) * 2 + x, (1 - y) * 2 + 1 - x
    other = (dp, z * 2 + 1 - core)
    x_dev, y_dev = (x_dp, expert), (y_dp, expert)
    z_devs = [(dp, (z + k) % 4 * 2 + core) for k in range(1, 4)]
    cross = [(dp, (z + k) % 4 * 2 + 1 - core) for k in range(1, 4)]
    enter([other, x_dev, y_dev] + z_devs + cross)

    def block(dp_at, k, low=0, count=rows):
        at = ((z + 4 - k) % 4 * 2 + core) * rows + low
        return out_ref.at[pl.ds(at, count), pl.ds(dp_at * cols, cols)]

    def copy(ref, dst, send, recv, device):
        return pltpu.make_async_remote_copy(
            src_ref=ref, dst_ref=dst, send_sem=send, recv_sem=recv, device_id=device, device_id_type=MESH
        )

    weights = (pltpu.make_async_copy(gate_ref, gate_w, gw_sem), pltpu.make_async_copy(up_ref, up_w, uw_sem))
    sent = []

    def go(*args):
        c = copy(*args)
        c.start()
        sent.append(c)

    def arrived(dst, send, recv):
        copy(dst, dst, send, recv, other).wait_recv()

    own = pltpu.make_async_copy(tok_ref, block(dp, 0), own_sem)
    own.start()

    def table_at(k, side):
        return tabs_ref.at[pl.ds(((z + 4 - k) % 4 * 2 + side) * rows, rows), :]

    own_tab = pltpu.make_async_copy(tab_ref, table_at(0, core), tab_sem)
    own_tab.start()
    go(tok_ref, block(dp, 0), x_send.at[0], x_recv.at[0], x_dev)
    go(tok_ref, block(dp, 0), y_send.at[0], y_recv.at[0], y_dev)
    for k in range(1, 4):
        go(tok_ref, block(dp, 0), z_send.at[k - 1], z_recv.at[k - 1], z_devs[k - 1])
    go(tok_ref, block(dp, 0), s_send.at[0], s_recv.at[0], other)
    for i, device in enumerate([other] + z_devs + cross):
        go(tab_ref, table_at(0, core), t_send.at[i], t_recv.at[i], device)

    def near(k):
        arrived(block(x_dp, k), x_send.at[k], x_recv.at[k])
        go(block(x_dp, k, 0, half), block(x_dp, k, 0, half), dy_send.at[k], dy_recv.at[k], y_dev)
        go(block(x_dp, k), block(x_dp, k), s_send.at[4 + k], s_recv.at[4 + k], other)
        arrived(block(y_dp, k), y_send.at[k], y_recv.at[k])
        go(block(y_dp, k, half, half), block(y_dp, k, half, half), dx_send.at[k], dx_recv.at[k], x_dev)
        go(block(y_dp, k), block(y_dp, k), s_send.at[8 + k], s_recv.at[8 + k], other)

    def far(k):
        arrived(block(d_dp, k, 0, half), dy_send.at[k], dy_recv.at[k])
        arrived(block(d_dp, k, half, half), dx_send.at[k], dx_recv.at[k])
        go(block(d_dp, k), block(d_dp, k), s_send.at[12 + k], s_recv.at[12 + k], other)

    def column(k):
        arrived(block(dp, k), z_send.at[k - 1], z_recv.at[k - 1])
        go(block(dp, k), block(dp, k), x_send.at[k], x_recv.at[k], x_dev)
        go(block(dp, k), block(dp, k), y_send.at[k], y_recv.at[k], y_dev)
        go(block(dp, k), block(dp, k), s_send.at[k], s_recv.at[k], other)

    for c in weights:
        c.start()
    columns_of = (dp, x_dp, y_dp, d_dp)

    def pair(j, k):
        at = ((z + 4 - k) % 4 * 2 + 1 - core) * rows
        col = pl.multiple_of(columns_of[j] * cols, cols)
        arrived(out_ref.at[pl.ds(at, rows), pl.ds(col, cols)], s_send.at[4 * j + k], s_recv.at[4 * j + k])
        both = pl.ds(pl.multiple_of((z + 4 - k) % 4 * 2 * rows, 2 * rows), 2 * rows)
        piece = out_ref[both, pl.ds(col, cols)]
        for acc, matrix in ((gate_acc, gate_w), (up_acc, up_w)):
            value = jnp.dot(piece, matrix[pl.ds(col, cols), :], preferred_element_type=jnp.float32)
            acc[both, :] = value if j == 0 else acc[both, :] + value

    def finish(k):
        both = pl.ds(pl.multiple_of((z + 4 - k) % 4 * 2 * rows, 2 * rows), 2 * rows)
        gate = gate_acc[both, :]
        value = gate / (1.0 + jnp.exp(-gate)) * up_acc[both, :]
        hid_ref[both, :] = jnp.where(w_ref[both, :] > 0, value, 0.0).astype(hid_ref.dtype)

    column(1)
    near(0)
    column(3)
    own.wait()
    for c in weights:
        c.wait()
    pair(0, 0)
    column(2)
    pair(1, 0)
    pair(2, 0)
    pair(0, 1)
    near(1)
    far(0)
    own_tab.wait()
    for i in range(7):
        k, side = (0, 1 - core) if i == 0 else (i, core) if i < 4 else (i - 3, 1 - core)
        arrived(table_at(k, side), t_send.at[i], t_recv.at[i])
    experts = lax.broadcasted_iota(jnp.int32, tabs_ref.shape, 1)
    w_ref[...] = jnp.sum(jnp.where(experts == expert, tabs_ref[...], 0.0), axis=1, keepdims=True)
    pair(0, 3)
    pair(0, 2)
    near(3)
    far(1)
    pair(3, 0)
    finish(0)
    pair(1, 1)
    pair(2, 1)
    near(2)
    far(3)
    pair(3, 1)
    finish(1)
    pair(1, 3)
    pair(2, 3)
    far(2)
    pair(3, 3)
    finish(3)
    pair(1, 2)
    pair(2, 2)
    pair(3, 2)
    finish(2)
    for c in sent:
        c.wait_send()


def hidden_units(tokens, table, gate, up):
    rows, cols = tokens.shape
    dma, vmem = pltpu.SemaphoreType.DMA, pltpu.VMEM
    units = gate.shape[1]
    return pl.pallas_call(
        hidden_kernel,
        out_shape=(
            jax.ShapeDtypeStruct((rows * 8, units), tokens.dtype),
            jax.ShapeDtypeStruct((rows * 8, 1), table.dtype),
        ),
        in_specs=[pl.BlockSpec(memory_space=pltpu.VMEM)] * 2 + [pl.BlockSpec(memory_space=pl.ANY)] * 2,
        out_specs=(pl.BlockSpec(memory_space=pltpu.VMEM),) * 2,
        scratch_shapes=[
            vmem((rows * 8, cols * 4), tokens.dtype),
            vmem((rows * 8, table.shape[1]), table.dtype),
            vmem(gate.shape, gate.dtype),
            vmem(up.shape, up.dtype),
            vmem((rows * 8, units), jnp.float32),
            vmem((rows * 8, units), jnp.float32),
        ]
        + [dma] * 4
        + [dma((7,))] * 2
        + [dma((3,))] * 2
        + [dma((4,))] * 8
        + [dma((16,))] * 2,
        compiler_params=pltpu.CompilerParams(collective_id=0, has_side_effects=True, vmem_limit_bytes=VMEM_BYTES),
    )(tokens, table, gate, up)


def combine_kernel(hid_ref, down_ref, basis_ref, w_ref, out_ref, sketch_ref, work, sbuf, rbuf, pbuf, dxb, dyb, xb, yb, zb, zr, zs, zn, z2, zz,
                   s_send, s_recv, dx_send, dx_recv, dy_send, dy_recv, x_send, x_recv, y_send, y_recv, z_send, z_recv, q_send, q_recv):
    dp, expert, y, x, z, core = place()
    rows, cols = out_ref.shape
    half = rows // 2
    x_dp, y_dp, d_dp = y * 2 + 1 - x, (1 - y) * 2 + x, (1 - y) * 2 + 1 - x
    targets = (dp, x_dp, y_dp, d_dp)
    other = (dp, z * 2 + 1 - core)
    x_dev, y_dev = (x_dp, expert), (y_dp, expert)
    z_devs = [(dp, (z + k) % 4 * 2 + core) for k in range(1, 4)]
    enter([other, x_dev, y_dev] + z_devs)

    def copy(ref, dst, send, recv, device):
        return pltpu.make_async_remote_copy(
            src_ref=ref, dst_ref=dst, send_sem=send, recv_sem=recv, device_id=device, device_id_type=MESH
        )

    def q_copy(i, ref, dst, device):
        return copy(ref, dst, q_send.at[i], q_recv.at[i], device)

    count = zs.shape[0] // 2
    lo, hi = pl.ds(0, count), pl.ds(count, count)
    zs[...] = jnp.dot(hid_ref[...], basis_ref[...], preferred_element_type=jnp.float32).astype(zs.dtype)
    q = [
        q_copy(0, zs.at[lo], zn.at[lo], x_dev),
        q_copy(1, zs.at[hi], zn.at[hi], y_dev),
        q_copy(2, z2.at[lo], zz.at[lo], y_dev),
        q_copy(3, z2.at[hi], zz.at[hi], x_dev),
    ]
    q[0].start()
    q[1].start()

    def product(k, j, side):
        at = pl.multiple_of(((z + k) % 4 * 2 + side) * rows, rows)
        col = pl.multiple_of(targets[j] * cols, cols)
        dot = jnp.dot(hid_ref[pl.ds(at, rows), :], down_ref[:, pl.ds(col, cols)], preferred_element_type=jnp.float32)
        return dot * w_ref[pl.ds(at, rows), :]

    def s_copy(k, j):
        return copy(sbuf.at[k, j], rbuf.at[k, j], s_send.at[k, j], s_recv.at[k, j], other)

    def dx_copy(k):
        return copy(pbuf.at[k, 3, pl.ds(0, half)], dxb.at[k], dx_send.at[k], dx_recv.at[k], x_dev)

    def dy_copy(k):
        return copy(pbuf.at[k, 3, pl.ds(half, half)], dyb.at[k], dy_send.at[k], dy_recv.at[k], y_dev)

    def x_copy(k):
        return copy(pbuf.at[k, 1], xb.at[k], x_send.at[k], x_recv.at[k], x_dev)

    def y_copy(k):
        return copy(pbuf.at[k, 2], yb.at[k], y_send.at[k], y_recv.at[k], y_dev)

    def z_copy(k):
        return copy(zb.at[k - 1], zr.at[k - 1], z_send.at[k - 1], z_recv.at[k - 1], z_devs[k - 1])

    order = (2, 1, 3, 0)

    def give(k, j):
        sbuf[k, j] = product(k, j, 1 - core).astype(sbuf.dtype)
        s_copy(k, j).start()

    def own(k, j):
        mine = product(k, j, core)
        s_copy(k, j).wait_recv()
        pbuf[k, j] = (mine + rbuf[k, j].astype(jnp.float32)).astype(pbuf.dtype)

    for k in order:
        give(k, 3)
    for k in order:
        own(k, 3)
        dx_copy(k).start()
        dy_copy(k).start()
    for k in order:
        give(k, 2)
        give(k, 1)
    for i, part in ((0, lo), (1, hi)):
        q[i].wait_recv()
        z2[part, :] = (zs[part, :].astype(jnp.float32) + zn[part, :].astype(jnp.float32)).astype(z2.dtype)
        q[2 + i].start()

    def second(k):
        dx_copy(k).wait_recv()
        pbuf[k, 2, 0:half] = (pbuf[k, 2, 0:half].astype(jnp.float32) + dxb[k].astype(jnp.float32)).astype(pbuf.dtype)
        y_copy(k).start()
        dy_copy(k).wait_recv()
        pbuf[k, 1, half:rows] = (pbuf[k, 1, half:rows].astype(jnp.float32) + dyb[k].astype(jnp.float32)).astype(pbuf.dtype)
        x_copy(k).start()

    def third(k):
        x_copy(k).wait_recv()
        y_copy(k).wait_recv()
        return pbuf[k, 0].astype(jnp.float32) + xb[k].astype(jnp.float32) + yb[k].astype(jnp.float32)

    def fourth(k):
        zb[k - 1] = third(k).astype(zb.dtype)
        z_copy(k).start()

    for k in order:
        own(k, 2)
        own(k, 1)
        second(k)
    for k in order:
        give(k, 0)
    for k in order:
        own(k, 0)
    q[2].wait_recv()
    q[3].wait_recv()
    q[0].wait_send()
    q[1].wait_send()
    zs[...] = (z2[...].astype(jnp.float32) + zz[...].astype(jnp.float32)).astype(zs.dtype)
    sk = work.shape[0]
    panel_rows = 32
    contract = (((0,), (0,)), ((), ()))
    line = lax.broadcasted_iota(jnp.int32, (sk, sk), 0)
    eye = (line == lax.broadcasted_iota(jnp.int32, (sk, sk), 1)).astype(jnp.float32)
    work[:, 0:sk] = lax.dot_general(zs[...], zs[...], contract, preferred_element_type=jnp.float32) + ridge_term * eye
    work[:, sk:] = eye

    def eliminate(p):
        low = p * panel_rows
        lanes = lax.broadcasted_iota(jnp.int32, (panel_rows, 2 * sk), 1)
        lines = lax.broadcasted_iota(jnp.int32, (panel_rows, 2 * sk), 0)

        def step(r, panel):
            row = jnp.sum(jnp.where(lines == r, panel, 0.0), axis=0, keepdims=True)
            column = jnp.sum(jnp.where(lanes[:, :sk] == low + r, panel[:, :sk], 0.0), axis=1, keepdims=True)
            pivot = jnp.sum(jnp.where(lanes[0:1, :sk] == low + r, row[:, :sk], 0.0), axis=1, keepdims=True)
            scale = lax.rsqrt(pivot)
            row = row * scale
            below = panel - (column * scale) * row
            return jnp.where(lines < r, panel, jnp.where(lines == r, row, below))

        panel = lax.fori_loop(0, panel_rows, step, work[low : low + panel_rows, :])
        work[low : low + panel_rows, :] = panel
        high = low + panel_rows
        if high < sk:
            update = lax.dot_general(
                panel[:, :sk], panel, contract, precision=lax.Precision.HIGHEST, preferred_element_type=jnp.float32
            )
            work[high:, :] = work[high:, :] - update[high:, :]

    fourth(2)
    eliminate(0)
    fourth(1)
    eliminate(1)
    fourth(3)
    eliminate(2)
    eliminate(3)
    total = third(0)
    projected = lax.dot_general(zs[...], hid_ref[...], contract, preferred_element_type=jnp.float32)
    sketch_ref[...] = jnp.dot(
        work[:, sk:], projected, precision=lax.Precision.HIGHEST, preferred_element_type=jnp.float32
    )
    for k in (2, 1, 3):
        z_copy(k).wait_recv()
        total = total + zr[k - 1].astype(jnp.float32)
    out_ref[...] = total.astype(out_ref.dtype)
    for c in q[2:]:
        c.wait_send()
    for k in range(4):
        for j in range(4):
            s_copy(k, j).wait_send()
        for c in (dx_copy, dy_copy, x_copy, y_copy):
            c(k).wait_send()
        if k:
            z_copy(k).wait_send()


def combine(hidden, down, basis, weight, rows, cols):
    total, sk = hidden.shape[0], basis.shape[1]
    dma, vmem, kind = pltpu.SemaphoreType.DMA, pltpu.VMEM, jnp.bfloat16
    spec = pl.BlockSpec(memory_space=pltpu.VMEM)
    return pl.pallas_call(
        combine_kernel,
        out_shape=(jax.ShapeDtypeStruct((rows, cols), kind), jax.ShapeDtypeStruct((sk, hidden.shape[1]), jnp.float32)),
        in_specs=[spec] * 4,
        out_specs=(spec, spec),
        scratch_shapes=[vmem((sk, 2 * sk), jnp.float32)]
        + [vmem((4, 4, rows, cols), kind)] * 3
        + [vmem((4, rows // 2, cols), kind)] * 2
        + [vmem((4, rows, cols), kind)] * 2
        + [vmem((3, rows, cols), kind)] * 2
        + [vmem((total, sk), kind)] * 4
        + [dma((4, 4))] * 2
        + [dma((4,))] * 8
        + [dma((3,))] * 2
        + [dma((4,))] * 2,
        compiler_params=pltpu.CompilerParams(collective_id=1, has_side_effects=True, vmem_limit_bytes=VMEM_BYTES),
    )(hidden, down, basis, weight)


def dense_body(tokens, routes, route_weights, gate_weight, up_weight, down_weight, sketch_basis):
    owners = lax.axis_size("expert")
    experts = jnp.arange(owners, dtype=jnp.int32)
    table = jnp.sum(jnp.where(routes[:, :, None] == experts, route_weights[:, :, None], 0.0), axis=1)
    hidden, weight = hidden_units(tokens, table, gate_weight[0], up_weight[0])
    mixed, whitened = combine(hidden, down_weight[0], sketch_basis, weight, *tokens.shape)
    return (mixed, whitened[None])


def solution(mesh):
    dense = mesh.shape["dp"] == 4 and mesh.shape["expert"] == 8
    return jax.shard_map(
        dense_body if dense else body,
        mesh=mesh,
        in_specs=(
            P("expert", "dp"),
            P("expert", None),
            P("expert", None),
            P("expert", None, "dp"),
            P("expert", None, "dp"),
            P("expert", "dp", None),
            P("dp", None),
        ),
        out_specs=(P("expert", "dp"), P("expert", None, "dp")),
        check_vma=False,
    )
```
